32 devices in a mesh: group: 2 (over x), wide: 16 (over z, y, core).
Axes of the slice: x: 2, y: 2, z: 4, core: 2. Of those that a mesh axis runs over, the one named last changes fastest.
Arguments:
- residual: bfloat16 [64, 16384], P('group', 'wide'), parts along dimension 0, may hold values from -4 to 4
- norm_gain: bfloat16 [16384], P('wide'), may hold values from 0.25 to 1.75
- w_qkv: bfloat16 [16384, 9216], P('wide'), may hold values from -1 to 1
- w_out: bfloat16 [8192, 16384], P(None, 'wide'), may hold values from -16 to 16
- cached_key_rows: bfloat16 [64, 512, 512], P(('group', 'wide')), parts along dimension 0, may hold values from -256 to 256
- cached_value_rows: bfloat16 [64, 512, 512], P(('group', 'wide')), parts along dimension 0, may hold values from -6 to 6
- lengths: int32 [64], P(('group', 'wide')), parts along dimension 0, may hold values from 32 to 512, as said below
Outputs:
- branch: bfloat16 [2, 64, 16384], P(None, 'group', 'wide'), parts along dimension 1
- fresh_kv: bfloat16 [64, 2, 1024], P(('group', 'wide')), parts along dimension 0
The draws below stay inside these ranges and needn't reach their ends.
There are 2 independent parts, one for each index of `group`. The reference program is written for one: setup_inputs(seed, part) draws one part's arguments, and reference() takes and returns one part's arrays. A program takes and returns all parts, laid end to end along the dimension named above; an argument that names none is the same for every part. Nothing has to cross between parts.
Inputs may be any that keep to these rules, and one draw needn't show every extreme that they name: `lengths`: one sequence in every draw fills all 512 slots.
All inputs are finite; a program needn't handle non-finite values.
Results may differ from the reference program's by a relative error of at most 0.019.
Values may be sent and summed in bfloat16 or wider, within the bound.
A program may use at most 128 MiB of HBM per device.

```python
import math
import jax
import jax.numpy as jnp
from jax import lax

D = 16384
QUERY_HEADS = 64
KEY_VALUE_HEADS = 4
HEAD_SIZE = 128
CACHE_SLOTS = 512
DECODE_STEPS = 2
BATCH_ROWS = 32
QKV = 9216


LEVEL_NORM = math.sqrt((10.0 ** 0.8 - 10.0 ** (-0.8)) / (1.6 * math.log(10.0)))


def feature_levels(key):
    level_key = jax.random.fold_in(key, 91)
    return 10.0 ** jax.random.uniform(level_key, (D,), jnp.float32, -0.4, 0.4)


def draw_residual(key, part):
    key = jax.random.fold_in(key, 11)
    subkeys = jax.random.split(key, 3)
    column_index = jnp.arange(D, dtype=jnp.float32)[None, :]
    col_scale = 10.0 ** jax.random.uniform(subkeys[1], (1, D), jnp.float32)
    row_scale = 10.0 ** jax.random.uniform(subkeys[0], (BATCH_ROWS, 1), jnp.float32)
    trend = 3.0 ** (0.5 * column_index / D)
    bulk_values = jnp.clip(jax.random.normal(subkeys[2], (BATCH_ROWS, D), jnp.float32), -4.0, 4.0)
    overall = 0.005
    return (bulk_values * row_scale * col_scale * trend * overall).astype(jnp.bfloat16)


def draw_w_qkv(key, part):
    levels = feature_levels(key)
    key = jax.random.fold_in(key, 41)
    row_factor = 1.0 / (levels * LEVEL_NORM)
    noise_part = jnp.clip(jax.random.normal(key, (D, QKV), jnp.float32), -4.0, 4.0)
    return (noise_part * row_factor[:, None] * (1.0 / math.sqrt(D))).astype(jnp.bfloat16)


def draw_w_out(key, part):
    levels = feature_levels(key)
    key = jax.random.fold_in(key, 53)
    subkeys = jax.random.split(key, 3)
    inner_width = QUERY_HEADS * HEAD_SIZE
    fan_value = max(inner_width // 32, 1)
    noise_part = jnp.clip(jax.random.normal(subkeys[0], (inner_width, D), jnp.float32), -4.0, 4.0)
    row_factor = jnp.clip(jax.random.normal(subkeys[1], (inner_width,), jnp.float32), -3.0, 3.0)
    column_factor = jnp.clip(jax.random.normal(subkeys[2], (D,), jnp.float32), -3.0, 3.0)
    combined = noise_part + row_factor[:, None] * column_factor[None, :]
    column_scale = levels / LEVEL_NORM
    return (combined * column_scale[None, :] * (1.0 / math.sqrt(2.0 * fan_value))).astype(jnp.bfloat16)


def draw_cached_key_rows(key, part):
    key = jax.random.fold_in(key, 23)
    subkeys = jax.random.split(key, 1)
    model_width = KEY_VALUE_HEADS * HEAD_SIZE
    bulk_values = jnp.clip(jax.random.normal(subkeys[0], (BATCH_ROWS, CACHE_SLOTS, model_width), jnp.float32), -4.0, 4.0)
    return bulk_values.astype(jnp.bfloat16)


def draw_lengths(key, part):
    key = jax.random.fold_in(key, 37)
    subkeys = jax.random.split(key, 2)
    length_draw = jax.random.randint(subkeys[0], (BATCH_ROWS,), max(2, CACHE_SLOTS // 16), CACHE_SLOTS + 1, dtype=jnp.int32)
    longest = jax.random.randint(subkeys[1], (), 0, BATCH_ROWS, dtype=jnp.int32)
    return jnp.where(jnp.arange(BATCH_ROWS, dtype=jnp.int32) == longest, CACHE_SLOTS, length_draw).astype(jnp.int32)


def shard_levels(stream_key, dims, cuts, smallest, high):
    level = 1.0
    for position, blocks in cuts:
        heights = jax.random.uniform(jax.random.fold_in(jax.random.fold_in(stream_key, 6), position), (blocks,), jnp.float32, smallest / len(cuts), high / len(cuts))
        level = level * jnp.repeat(jnp.exp(heights), dims[position] // blocks).reshape((-1,) + (1,) * (len(dims) - 1 - position))
    return level


def noise(rng, extent, width, limit, pieces=(), kind=jnp.bfloat16):
    array = width * jax.random.normal(rng, extent, jnp.float32)
    if pieces:
        array = array * shard_levels(rng, extent, pieces, -0.22, 0.18)
    return jnp.clip(array, -limit, limit).astype(kind)


def setup_inputs(seed: int = 0, part: int = 0) -> dict:
    arg_keys = jax.random.split(jax.random.key(seed), 8)
    own_keys = jax.random.split(jax.random.fold_in(arg_keys[7], part), 8)
    residual = draw_residual(jax.random.fold_in(jax.random.fold_in(arg_keys[7], part), 71), part)
    norm_gain = jnp.clip(1.0 + 0.15 * jax.random.normal(arg_keys[1], (D,), jnp.float32), 0.25, 1.75).astype(jnp.bfloat16)
    w_qkv = draw_w_qkv(jax.random.fold_in(arg_keys[7], 71), part)
    w_out = draw_w_out(jax.random.fold_in(arg_keys[7], 71), part)
    cached_key_rows = draw_cached_key_rows(jax.random.fold_in(jax.random.fold_in(arg_keys[7], part), 71), part)
    cached_value_rows = noise(own_keys[5], (BATCH_ROWS, CACHE_SLOTS, KEY_VALUE_HEADS * HEAD_SIZE), 1.0, 6.0, ((0, 16),))
    lengths = draw_lengths(jax.random.fold_in(jax.random.fold_in(arg_keys[7], part), 71), part)
    return {"residual": residual, "norm_gain": norm_gain, "w_qkv": w_qkv, "w_out": w_out, "cached_key_rows": cached_key_rows, "cached_value_rows": cached_value_rows, "lengths": lengths}


EPSILON = 1e-05

def apply_rotation(vectors, token_position):
    half_width = vectors.shape[-1] // 2
    frequency = 500000.0 ** (-(jnp.arange(half_width, dtype=jnp.float32) * (2.0 / vectors.shape[-1])))
    angles = token_position.astype(jnp.float32)[:, None, None] * frequency
    cosine = jnp.cos(angles)
    sine_part = jnp.sin(angles)
    first_half = vectors[..., :half_width]
    second_half = vectors[..., half_width:]
    return jnp.concatenate([first_half * cosine - second_half * sine_part, first_half * sine_part + second_half * cosine], axis=-1)

def attend(query_rows, keys_grouped, values_grouped, lengths, new_keys, new_values):
    scaling = 1.0 / HEAD_SIZE ** 0.5
    cache_scores = jnp.einsum('bkgd,bpkd->bkgp', query_rows.astype(jnp.float32), keys_grouped.astype(jnp.float32)) * scaling
    visible = jnp.arange(CACHE_SLOTS, dtype=jnp.int32)[None, :] < lengths[:, None]
    cache_scores = jnp.where(visible[:, None, None, :], cache_scores, -jnp.inf)
    new_scores = jnp.einsum('bkgd,bktd->bkgt', query_rows.astype(jnp.float32), new_keys.astype(jnp.float32)) * scaling
    peak = jnp.maximum(lax.optimization_barrier(jnp.max(cache_scores, axis=-1)), lax.optimization_barrier(jnp.max(new_scores, axis=-1)))
    cache_exp = jnp.exp(cache_scores - peak[..., None])
    new_exp = jnp.exp(new_scores - peak[..., None])
    denominator = lax.optimization_barrier(jnp.sum(cache_exp, axis=-1)) + lax.optimization_barrier(jnp.sum(new_exp, axis=-1))
    weighted = jnp.einsum('bkgp,bpkd->bkgd', cache_exp.astype(jnp.bfloat16).astype(jnp.float32), values_grouped.astype(jnp.float32))
    weighted = weighted + jnp.einsum('bkgt,bktd->bkgd', new_exp.astype(jnp.bfloat16).astype(jnp.float32), new_values.astype(jnp.float32))
    result = (weighted / denominator[..., None]).astype(jnp.bfloat16)
    return result.reshape(result.shape[0], QUERY_HEADS * HEAD_SIZE)

def reference(residual, norm_gain, w_qkv, w_out, cached_key_rows, cached_value_rows, lengths):
    keys_grouped = cached_key_rows.reshape(BATCH_ROWS, CACHE_SLOTS, KEY_VALUE_HEADS, HEAD_SIZE)
    values_grouped = cached_value_rows.reshape(BATCH_ROWS, CACHE_SLOTS, KEY_VALUE_HEADS, HEAD_SIZE)
    hidden = residual
    key_collection = []
    value_collection = []
    branches = []
    for step_index in range(DECODE_STEPS):
        values_f = hidden.astype(jnp.float32)
        mean_square = lax.optimization_barrier(jnp.sum(values_f * values_f, axis=1)) / D
        gained = (values_f * norm_gain.astype(jnp.float32)).astype(jnp.bfloat16)
        projected_rows = jnp.dot(gained, w_qkv, preferred_element_type=jnp.float32) * lax.rsqrt(mean_square + EPSILON)[:, None]
        token_position = lengths + step_index
        query_rows = apply_rotation(projected_rows[:, :QUERY_HEADS * HEAD_SIZE].reshape(BATCH_ROWS, QUERY_HEADS, HEAD_SIZE), token_position).astype(jnp.bfloat16)
        query_rows = query_rows.reshape(BATCH_ROWS, KEY_VALUE_HEADS, QUERY_HEADS // KEY_VALUE_HEADS, HEAD_SIZE)
        incoming_key = apply_rotation(projected_rows[:, QUERY_HEADS * HEAD_SIZE:(QUERY_HEADS + KEY_VALUE_HEADS) * HEAD_SIZE].reshape(BATCH_ROWS, KEY_VALUE_HEADS, HEAD_SIZE), token_position).astype(jnp.bfloat16)
        incoming_value = projected_rows[:, (QUERY_HEADS + KEY_VALUE_HEADS) * HEAD_SIZE:].reshape(BATCH_ROWS, KEY_VALUE_HEADS, HEAD_SIZE).astype(jnp.bfloat16)
        key_collection.append(incoming_key)
        value_collection.append(incoming_value)
        attended = attend(query_rows, keys_grouped, values_grouped, lengths, jnp.stack(key_collection, axis=2), jnp.stack(value_collection, axis=2))
        mixed = jnp.dot(attended, w_out, preferred_element_type=jnp.float32).astype(jnp.bfloat16)
        branches.append(mixed)
        hidden = (values_f + mixed.astype(jnp.float32)).astype(jnp.bfloat16)
    fresh_entries = jnp.stack([jnp.concatenate([key_collection[step_number].reshape(BATCH_ROWS, KEY_VALUE_HEADS * HEAD_SIZE), value_collection[step_number].reshape(BATCH_ROWS, KEY_VALUE_HEADS * HEAD_SIZE)], axis=1) for step_number in range(DECODE_STEPS)], axis=1)
    return (jnp.stack(branches, axis=0), fresh_entries)
```

```python
import jax
import jax.numpy as jnp
from jax import lax
from jax.experimental import pallas as pl
from jax.experimental.pallas import tpu as pltpu
from jax.sharding import PartitionSpec as P

QUERY_HEADS = 64
KEY_VALUE_HEADS = 4
HEAD_SIZE = 128
DECODE_STEPS = 2
EPSILON = 1e-05
ROPE_BASE = 500000.0

GROUP_HEADS = QUERY_HEADS // KEY_VALUE_HEADS
HEADS_WIDTH = QUERY_HEADS * HEAD_SIZE
PAIR_HEADS = 2 * KEY_VALUE_HEADS
CHUNKS = [(QUERY_HEADS, PAIR_HEADS)] + [
    (k * GROUP_HEADS, GROUP_HEADS) for k in range(KEY_VALUE_HEADS)
]
ROW0 = [0] + [2 * PAIR_HEADS + 2 * k * GROUP_HEADS for k in range(KEY_VALUE_HEADS)]
LAST_CHUNK = len(CHUNKS) - 1
MESSAGE_ROWS = 2 * (QUERY_HEADS + PAIR_HEADS)
TILE = 512
MESH = pl.DeviceIdType.MESH
F32 = jnp.float32
BF16 = jnp.bfloat16


def semaphore_names(depth):
    names = []
    for t in range(DECODE_STEPS):
        names += [("q", t, 1), ("q", t, 2)]
        names += [("q", t, 3, r) for r in range(1, depth)]
        for j in range(len(CHUNKS)):
            names += [("p", t, j, 1), ("p", t, j, 2)]
            names += [("p", t, j, 3, r) for r in range(1, depth)]
        names += [("p", t, LAST_CHUNK, 3, r) for r in range(depth, 2 * depth)]
        for k in range(KEY_VALUE_HEADS):
            names += [("g", t, k, 2), ("g", t, k, 1)]
            names += [("g", t, k, 3, r) for r in range(1, depth)]
        names += [("g", t, LAST_CHUNK - 1, 3, r) for r in range(depth, 2 * depth)]
    return {name: index for index, name in enumerate(names)}


def make_kernel(n):
    depth = n // 4
    rows = 2 * n
    half = n
    quarter = n // 2
    sems = semaphore_names(depth)
    block = 2 * GROUP_HEADS

    def kernel(
        len_ref, x_ref, gain_ref, wq_hbm, wo_hbm, k_hbm, v_hbm,
        branch_ref, fresh_ref,
        wq, wo, keys, values,
        own, s1, r1, s2, r2, folded, s3, r3,
        sq, gathered, wide_f, lhs, acc, hidden,
        load_sem, send_sem, recv_sem,
    ):
        me = lax.axis_index("wide")
        my_a = me // 4
        my_b = (me // 2) % 2
        my_c = me % 2
        core_peer = {"wide": my_a * 4 + my_b * 2 + (1 - my_c)}
        y_peer = {"wide": my_a * 4 + (1 - my_b) * 2 + my_c}
        z_peer = [
            {"wide": lax.rem(my_a + r, depth) * 4 + my_b * 2 + my_c} for r in range(depth)
        ] + [
            {"wide": lax.rem(my_a + r, depth) * 4 + (1 - my_b) * 2 + my_c} for r in range(depth)
        ]
        there = [(depth - r) % depth for r in range(depth)]
        there += [depth + r for r in there]

        def wq_copy(j):
            head, count = CHUNKS[j]
            columns = pl.ds(head * HEAD_SIZE, count * HEAD_SIZE)
            return pltpu.make_async_copy(wq_hbm.at[:, columns], wq.at[:, columns], load_sem.at[j])

        def wo_copy(k):
            part = pl.ds(k * GROUP_HEADS * HEAD_SIZE, GROUP_HEADS * HEAD_SIZE)
            return pltpu.make_async_copy(wo_hbm.at[part], wo.at[part], load_sem.at[7 + k])

        key_copy = pltpu.make_async_copy(k_hbm, keys, load_sem.at[5])
        value_copy = pltpu.make_async_copy(v_hbm, values, load_sem.at[6])
        for j in range(len(CHUNKS)):
            wq_copy(j).start()

        barrier = pltpu.get_barrier_semaphore()
        for peer in [core_peer] + z_peer[1:]:
            pl.semaphore_signal(barrier, inc=1, device_id=peer, device_id_type=MESH)

        copies = {}

        def send(name, src, dst, peer):
            copy = pltpu.make_async_remote_copy(
                src_ref=src,
                dst_ref=dst,
                send_sem=send_sem.at[sems[name]],
                recv_sem=recv_sem.at[sems[name]],
                device_id=peer,
                device_id_type=MESH,
            )
            copy.start()
            copies[name] = copy

        position = lax.broadcasted_iota(jnp.int32, (rows, rows), 0)
        natural = lax.broadcasted_iota(jnp.int32, (rows, rows), 1)
        s_pos = position % 2
        a_pos = (my_a + (position // 2) % depth) % depth
        b_pos = (my_b + (position // quarter) % 2) % 2
        c_pos = (my_c + position // half) % 2
        row_of = 2 * (4 * a_pos + 2 * b_pos + c_pos) + s_pos
        arrange = (row_of == natural).astype(F32).astype(BF16)
        diagonal = position == natural

        lane = lax.broadcasted_iota(jnp.int32, (1, HEAD_SIZE), 1)
        pair = lane % (HEAD_SIZE // 2)
        frequency = jnp.ones((1, HEAD_SIZE), F32)
        for bit in range(6):
            factor = ROPE_BASE ** (-(2.0 ** (bit + 1)) / HEAD_SIZE)
            frequency = frequency * jnp.where((pair // 2**bit) % 2 == 1, F32(factor), F32(1.0))
        tables = {}
        for t in range(DECODE_STEPS):
            for s in range(2):
                angle = (len_ref[s] + t).astype(F32) * frequency
                sine = jnp.sin(angle)
                tables[t, s] = (
                    jnp.cos(angle),
                    jnp.where(lane < HEAD_SIZE // 2, -sine, sine),
                )

        def rotate(vectors, t, s):
            cosine, sine = tables[t, s]
            return vectors * cosine + pltpu.roll(vectors, HEAD_SIZE // 2, 1) * sine

        slot = lax.broadcasted_iota(jnp.int32, (GROUP_HEADS, keys.shape[1]), 1)
        fresh_keys, fresh_values = {}, {}
        inverse = {}
        width = x_ref.shape[1] * n

        hidden[...] = x_ref[...]

        def start_step(t):
            x = hidden[...].astype(F32)
            squares = jnp.sum(x * x, axis=1, keepdims=True)
            line = jnp.sum(jnp.where(diagonal, squares, 0.0), axis=0, keepdims=True)
            if rows < HEAD_SIZE:
                line = jnp.concatenate([line] + [jnp.zeros((1, HEAD_SIZE - rows), F32)], axis=1)
            sq[t, 0] = jnp.broadcast_to(line, (8, HEAD_SIZE))
            gained = (x * gain_ref[...].astype(F32).reshape(1, -1)).astype(BF16)
            return jnp.dot(arrange, gained, preferred_element_type=F32).astype(BF16)

        def project(t, j, gained):
            head, count = CHUNKS[j]
            if t == 0:
                wq_copy(j).wait()

            def body(i, carry):
                columns = pl.ds(pl.multiple_of(head * HEAD_SIZE + i * TILE, TILE), TILE)
                part = jnp.dot(gained, wq[:, columns], preferred_element_type=F32)
                own[:, columns] = part[:half]
                s1[t, :, columns] = part[half:].astype(BF16)
                return carry

            lax.fori_loop(0, count * HEAD_SIZE // TILE, body, 0, unroll=2)
            if t == 0 and j == 0:
                pl.semaphore_wait(barrier, 2 * depth)
            if j == 0:
                send(("q", t, 1), sq.at[t, 0], sq.at[t, 1], core_peer)
            columns = pl.ds(head * HEAD_SIZE, count * HEAD_SIZE)
            send(("p", t, j, 1), s1.at[t, :, columns], r1.at[t, :, columns], core_peer)

        def send_sum(t, j, r):
            count = CHUNKS[j][1]
            place = pl.ds(ROW0[j], 2 * count)
            start = 2 * (r % depth)
            s3[t, r, place, :] = jnp.concatenate(
                [
                    folded[j + r // depth, pl.ds(start + s, count, stride=quarter), :]
                    for s in range(2)
                ],
                axis=0,
            ).astype(BF16)
            send(("p", t, j, 3, r), s3.at[t, r, place], r3.at[t, there[r], place], z_peer[r])

        def reduce_core(t, j):
            head, count = CHUNKS[j]
            if j == 0:
                copies["q", t, 1].wait_recv()
                sq[t, 2] = sq[t, 0] + sq[t, 1]
                send(("q", t, 2), sq.at[t, 2], sq.at[t, 3], y_peer)
            copies["p", t, j, 1].wait_recv()
            first, size = head * HEAD_SIZE, count * HEAD_SIZE
            columns = pl.ds(first, size)
            total = own[:, columns] + r1[t, :, columns].astype(F32)
            if j == LAST_CHUNK:
                for side in range(2):
                    for h in range(count):
                        folded[j + side, pl.ds(h * quarter, quarter), :] = total[
                            side * quarter : (side + 1) * quarter,
                            h * HEAD_SIZE : (h + 1) * HEAD_SIZE,
                        ]
                for r in range(depth, 2 * depth):
                    send_sum(t, j, r)
                for r in range(1, depth):
                    send_sum(t, j, r)
                return
            own[0:quarter, columns] = total[:quarter]
            away = total[quarter:]
            packed = pl.ds(first // 2, size // 2)
            s2[t, :, packed] = jnp.concatenate(
                [away[:, : size // 2], away[:, size // 2 :]], axis=0
            ).astype(BF16)
            send(("p", t, j, 2), s2.at[t, :, packed], r2.at[t, :, packed], y_peer)

        def reduce_y(t, j):
            head, count = CHUNKS[j]
            if j == 0:
                copies["q", t, 2].wait_recv()
                sq[t, 4] = sq[t, 2] + sq[t, 3]
                for r in range(1, depth):
                    send(("q", t, 3, r), sq.at[t, 4], sq.at[t, 4 + depth - r], z_peer[r])
            copies["p", t, j, 2].wait_recv()
            first, size = head * HEAD_SIZE, count * HEAD_SIZE
            arrived = r2[t, :, pl.ds(first // 2, size // 2)].astype(F32)
            for h in range(count):
                place = h * HEAD_SIZE
                if place < size // 2:
                    other = arrived[:quarter, place : place + HEAD_SIZE]
                else:
                    place -= size // 2
                    other = arrived[quarter:, place : place + HEAD_SIZE]
                folded[j, pl.ds(h * quarter, quarter), :] = (
                    own[0:quarter, pl.ds(first + h * HEAD_SIZE, HEAD_SIZE)] + other
                )
            for r in range(1, depth):
                send_sum(t, j, r)

        def reduce_z(t, j):
            head, count = CHUNKS[j]
            if j == 0:
                total = sq[t, 4]
                for r in range(1, depth):
                    copies["q", t, 3, r].wait_recv()
                for r in range(1, depth):
                    total = total + sq[t, 4 + r]
                line = total[0:1]
                for s in range(2):
                    mine = jnp.sum(
                        jnp.where(lane == 2 * me + s, line, 0.0), axis=1, keepdims=True
                    )
                    inverse[t, s] = lax.rsqrt(mine / width + EPSILON)
            others = range(1, 2 * depth if j == LAST_CHUNK else depth)
            for r in others:
                copies["p", t, j, 3, r].wait_recv()
            arrived = None
            for r in others:
                term = r3[t, r, pl.ds(ROW0[j], 2 * count), :].astype(F32)
                arrived = term if arrived is None else arrived + term
            result = []
            for s in range(2):
                mine = folded[j, pl.ds(s, count, stride=quarter), :]
                result.append((mine + arrived[s * count : (s + 1) * count]) * inverse[t, s])
            return result

        def finish_pair(t):
            both = reduce_z(t, 0)
            for s in range(2):
                rotated = rotate(both[s], t, s)
                fresh_keys[t, s] = rotated[:KEY_VALUE_HEADS].astype(BF16).astype(F32)
                fresh_values[t, s] = both[s][KEY_VALUE_HEADS:].astype(BF16).astype(F32)

        def attend(t, k):
            queries = reduce_z(t, k + 1)
            if t == 0 and k == 0:
                key_copy.wait()
                value_copy.wait()
            scaling = 1.0 / HEAD_SIZE**0.5
            columns = pl.ds(k * HEAD_SIZE, HEAD_SIZE)
            results = []
            for s in range(2):
                query = rotate(queries[s], t, s).astype(BF16)
                scores = lax.dot_general(
                    query, keys[s, :, columns], (((1,), (1,)), ((), ())),
                    preferred_element_type=F32,
                ) * scaling
                scores = jnp.where(slot < len_ref[s], scores, -jnp.inf)
                query_f = query.astype(F32)
                recent = [
                    jnp.sum(query_f * fresh_keys[u, s][k : k + 1], axis=1, keepdims=True) * scaling
                    for u in range(t + 1)
                ]
                peak = jnp.max(scores, axis=1, keepdims=True)
                for score in recent:
                    peak = jnp.maximum(peak, score)
                e = jnp.exp(scores - peak)
                denominator = jnp.sum(e, axis=1, keepdims=True)
                weighted = jnp.dot(e.astype(BF16), values[s, :, columns], preferred_element_type=F32)
                for u, score in enumerate(recent):
                    e_new = jnp.exp(score - peak)
                    denominator = denominator + e_new
                    weighted = (
                        weighted + e_new.astype(BF16).astype(F32) * fresh_values[u, s][k : k + 1]
                    )
                results.append(weighted / denominator)
            gathered[t, k, pl.ds(0, block), :] = jnp.concatenate(results, axis=0).astype(BF16)
            for r in range(1, 2 * depth if k + 1 == LAST_CHUNK else depth):
                send(
                    ("g", t, k, 3, r),
                    gathered.at[t, k, pl.ds(0, block)],
                    gathered.at[t, k, pl.ds(there[r] * block, block)],
                    z_peer[r],
                )

        def gather_y(t, k):
            for r in range(1, depth):
                copies["g", t, k, 3, r].wait_recv()
            size = depth * block
            send(
                ("g", t, k, 2),
                gathered.at[t, k, pl.ds(0, size)],
                gathered.at[t, k, pl.ds(size, size)],
                y_peer,
            )

        def gather_core(t, k):
            if k + 1 == LAST_CHUNK:
                for r in range(1, 2 * depth):
                    copies["g", t, k, 3, r].wait_recv()
            else:
                copies["g", t, k, 2].wait_recv()
            size = 2 * depth * block
            send(
                ("g", t, k, 1),
                gathered.at[t, k, pl.ds(0, size)],
                gathered.at[t, k, pl.ds(size, size)],
                core_peer,
            )

        def output(t, k):
            copies["g", t, k, 1].wait_recv()
            if t == 0:
                wo_copy(k).wait()
            wide_f[...] = gathered[t, k].astype(F32)
            for h in range(GROUP_HEADS):
                lhs[:, pl.ds(h * HEAD_SIZE, HEAD_SIZE)] = wide_f[
                    pl.ds(h, rows, stride=GROUP_HEADS), :
                ].astype(BF16)
            part = GROUP_HEADS * HEAD_SIZE
            tile = min(512, x_ref.shape[1])

            def body(i, carry):
                columns = pl.ds(pl.multiple_of(i * tile, tile), tile)
                term = jnp.dot(
                    lhs[...], wo[pl.ds(k * part, part), columns], preferred_element_type=F32
                )
                if k:
                    term = acc[:, columns] + term
                acc[:, columns] = term
                return carry

            lax.fori_loop(0, x_ref.shape[1] // tile, body, 0, unroll=True)

        def finish_step(t):
            mixed = acc[...].astype(BF16)
            natural_order = lax.dot_general(
                arrange, mixed, (((0,), (0,)), ((), ())), preferred_element_type=F32
            )
            branch_ref[t] = natural_order.astype(BF16)
            hidden[...] = (hidden[...].astype(F32) + natural_order).astype(BF16)

        for t in range(DECODE_STEPS):
            gained = start_step(t)
            project(t, 0, gained)
            project(t, 1, gained)
            reduce_core(t, 0)
            project(t, 2, gained)
            if t == 0:
                key_copy.start()
                value_copy.start()
                for k in range(KEY_VALUE_HEADS):
                    wo_copy(k).start()
            reduce_core(t, 1)
            project(t, 3, gained)
            reduce_core(t, 2)
            if t == 0:
                reduce_y(t, 0)
            project(t, 4, gained)
            reduce_core(t, 3)
            if t > 0:
                reduce_y(t, 0)
            reduce_core(t, 4)
            reduce_y(t, 1)
            reduce_y(t, 2)
            finish_pair(t)
            reduce_y(t, 3)
            attend(t, 0)
            attend(t, 1)
            gather_y(t, 0)
            attend(t, 2)
            gather_y(t, 1)
            attend(t, 3)
            gather_y(t, 2)
            gather_core(t, 0)
            gather_core(t, 1)
            output(t, 0)
            gather_core(t, 2)
            output(t, 1)
            gather_core(t, 3)
            output(t, 2)
            output(t, 3)
            finish_step(t)

        for s in range(2):
            lines = []
            for t in range(DECODE_STEPS):
                pieces = [
                    part[h : h + 1]
                    for part in (fresh_keys[t, s], fresh_values[t, s])
                    for h in range(KEY_VALUE_HEADS)
                ]
                lines.append(jnp.concatenate(pieces, axis=1))
            fresh_ref[s] = jnp.concatenate(lines, axis=0).astype(BF16)
        for copy in copies.values():
            copy.wait_send()

    return kernel, len(sems)


def solution(mesh):
    n = mesh.shape["wide"]
    depth = n // 4
    kernel, copies = make_kernel(n)

    def shards(residual, norm_gain, w_qkv, w_out, cached_key_rows, cached_value_rows, lengths):
        rows, width = residual.shape
        sequences = lengths.shape[0]
        columns = w_qkv.shape[1]
        chunks = len(CHUNKS)
        vmem = pl.BlockSpec(memory_space=pltpu.VMEM)
        hbm = pl.BlockSpec(memory_space=pl.ANY)
        branch, fresh = pl.pallas_call(
            kernel,
            out_shape=(
                jax.ShapeDtypeStruct((DECODE_STEPS, rows, width), BF16),
                jax.ShapeDtypeStruct((sequences, DECODE_STEPS, PAIR_HEADS * HEAD_SIZE), BF16),
            ),
            in_specs=[pl.BlockSpec(memory_space=pltpu.SMEM), vmem, vmem, hbm, hbm, hbm, hbm],
            out_specs=(vmem, vmem),
            scratch_shapes=[
                pltpu.VMEM(w_qkv.shape, BF16),
                pltpu.VMEM(w_out.shape, BF16),
                pltpu.VMEM(cached_key_rows.shape, BF16),
                pltpu.VMEM(cached_value_rows.shape, BF16),
                pltpu.VMEM((rows // 2, columns), F32),
                pltpu.VMEM((DECODE_STEPS, rows // 2, columns), BF16),
                pltpu.VMEM((DECODE_STEPS, rows // 2, columns), BF16),
                pltpu.VMEM((DECODE_STEPS, rows // 2, columns // 2), BF16),
                pltpu.VMEM((DECODE_STEPS, rows // 2, columns // 2), BF16),
                pltpu.VMEM((chunks + 1, GROUP_HEADS * rows // 4, HEAD_SIZE), F32),
                pltpu.VMEM((DECODE_STEPS, 2 * depth, MESSAGE_ROWS, HEAD_SIZE), BF16),
                pltpu.VMEM((DECODE_STEPS, 2 * depth, MESSAGE_ROWS, HEAD_SIZE), BF16),
                pltpu.VMEM((DECODE_STEPS, 4 + depth, 8, HEAD_SIZE), F32),
                pltpu.VMEM(
                    (DECODE_STEPS, KEY_VALUE_HEADS, rows * GROUP_HEADS, HEAD_SIZE), BF16
                ),
                pltpu.VMEM((rows * GROUP_HEADS, HEAD_SIZE), F32),
                pltpu.VMEM((rows, GROUP_HEADS * HEAD_SIZE), BF16),
                pltpu.VMEM((rows, width), F32),
                pltpu.VMEM((rows, width), BF16),
                pltpu.SemaphoreType.DMA((11,)),
                pltpu.SemaphoreType.DMA((copies,)),
                pltpu.SemaphoreType.DMA((copies,)),
            ],
            compiler_params=pltpu.CompilerParams(
                collective_id=0, has_side_effects=True, vmem_limit_bytes=56 * 1024 * 1024
            ),
            name="decode",
        )(
            lengths,
            residual,
            norm_gain,
            w_qkv,
            w_out,
            cached_key_rows,
            cached_value_rows,
        )
        return branch, fresh

    in_specs = (
        P("group", "wide"),
        P("wide"),
        P("wide", None),
        P(None, "wide"),
        P(("group", "wide"), None, None),
        P(("group", "wide"), None, None),
        P(("group", "wide")),
    )
    out_specs = (P(None, "group", "wide"), P(("group", "wide"), None, None))
    return jax.shard_map(shards, mesh=mesh, in_specs=in_specs, out_specs=out_specs, check_vma=False)
```
